1024 devices in a mesh: cell: 128 (over z, y), hour: 8 (over x, core).
Axes of the slice: x: 4, y: 4, z: 32, core: 2. Of those that a mesh axis runs over, the one named last changes fastest.
Arguments:
- slab: float32 [32768, 96, 256], P('cell', 'hour'), may hold values from -520 to 520
- start: float32 [256, 64], replicated, may hold values from -4 to 4
Outputs:
- subspace: float32 [256, 64], replicated
- hour_gram: float32 [96, 96], P('hour')
The draws below stay inside these ranges and needn't reach their ends.
All inputs are finite; a program needn't handle non-finite values.
Results may differ from the reference program's by a relative error of at most 0.0003.
Values sent between devices are 32-bit elements; how exact they have to be, the bound alone decides.
No kernel may reach another device: no remote copies, remote signals or barrier semaphores. Data moves between devices by JAX's collectives and lax.ppermute only.
A program may use at most 32 MiB of HBM per device.

```python
import math
import jax
import jax.numpy as jnp
from jax import lax

K = 256
H = 96
R = 64
POWER = 2
NC = 32768


def draw_slab(key, part):
    key = jax.random.fold_in(key, 11)
    key_cell = jax.random.fold_in(key, 0)
    key_kpi = jax.random.fold_in(key, 1)
    key_hour = jax.random.fold_in(key, 2)
    key_base = jax.random.fold_in(key, 3)
    key_factor = jax.random.fold_in(key, 5)
    cell_scale = jnp.exp(jax.random.uniform(key_cell, (NC, 1, 1), jnp.float32, jnp.log(0.3), jnp.log(3.0)))
    kpi_scale = jnp.exp(jax.random.uniform(key_kpi, (1, 1, K), jnp.float32, jnp.log(0.3), jnp.log(3.0)))
    hour_scale = jnp.exp(jax.random.uniform(key_hour, (1, H, 1), jnp.float32, jnp.log(0.6), jnp.log(1.8)))
    base = jax.random.truncated_normal(key_base, -4.0, 4.0, (NC, H, K), jnp.float32)
    wave_size = 0.8
    hour_index = jnp.arange(H, dtype=jnp.float32).reshape(1, H, 1)
    structure = jnp.zeros((NC, H, K), jnp.float32)
    for factor in range(4):
        key_load, key_prof, key_phase, key_kload = jax.random.split(jax.random.fold_in(key_factor, factor), 4)
        cell_load = jax.random.truncated_normal(key_load, -2.5, 2.5, (NC, 1, 1), jnp.float32)
        phase = jax.random.uniform(key_phase, (), jnp.float32, -math.pi, math.pi)
        rough = jax.random.truncated_normal(key_prof, -2.5, 2.5, (1, H, 1), jnp.float32)
        profile = wave_size * jnp.cos(hour_index * (2.0 * math.pi / 24.0) + phase) + 0.4 * rough
        kpi_load = jax.random.truncated_normal(key_kload, -2.5, 2.5, (1, 1, K), jnp.float32)
        structure = structure + 0.5 * cell_load * profile * kpi_load
    return (base + structure) * cell_scale * kpi_scale * hour_scale


def bell_draw(own_key, shape, spread, most, kind=jnp.bfloat16):
    entries = jax.random.normal(own_key, shape, jnp.float32) * spread
    return jnp.minimum(jnp.maximum(entries, -most), most).astype(kind)


def setup_inputs(seed: int = 0) -> dict:
    key_list = jax.random.split(jax.random.key(seed), 3)
    return {
        "slab": draw_slab(jax.random.fold_in(key_list[2], 71), 0),
        "start": bell_draw(key_list[1], (K, R), 1.0, 4.0, jnp.float32),
    }


def orthonormalize(columns):
    for repeat in range(2):
        inner_gram = jnp.dot(columns.T.astype(jnp.float32), columns.astype(jnp.float32), precision=lax.Precision.HIGHEST, preferred_element_type=jnp.float32)
        factor_low = jnp.linalg.cholesky(inner_gram)
        columns = jax.scipy.linalg.solve_triangular(factor_low, columns.T, lower=True).T
    return columns

def reference(slab, start):
    unfolded = slab.reshape(NC * H, K)
    kpi_gram = lax.dot_general(unfolded.astype(jnp.float32), unfolded.astype(jnp.float32), (((0,), (0,)), ((), ())), precision=lax.Precision.HIGHEST, preferred_element_type=jnp.float32) / (NC * H)
    subspace = start
    for repeat in range(POWER):
        subspace = orthonormalize(jnp.dot(kpi_gram.astype(jnp.float32), subspace.astype(jnp.float32), precision=lax.Precision.HIGHEST, preferred_element_type=jnp.float32))
    core_slab = jnp.dot(unfolded.astype(jnp.float32), subspace.astype(jnp.float32), precision=lax.Precision.HIGHEST, preferred_element_type=jnp.float32).reshape(NC, H, R)
    hour_gram = jnp.einsum('chr,cgr->hg', core_slab, core_slab, precision=lax.Precision.HIGHEST) / (NC * R)
    return (subspace, hour_gram)
```

```python
import functools

import jax
import jax.numpy as jnp
from jax import lax
from jax.experimental import pallas as pl
from jax.experimental.pallas import tpu as pltpu
from jax.sharding import Mesh, PartitionSpec as P

POWER = 2
F32 = jnp.float32
BF16 = jnp.bfloat16
HIGHEST = lax.Precision.HIGHEST
NEAR = ("y", "x", "core")
HOUR = ("x", "core")


def split(values):
    high = values.astype(BF16)
    low = (values - high.astype(F32)).astype(BF16)
    return high, low


def dot(a, b, contract):
    return lax.dot_general(a, b, (contract, ((), ())), preferred_element_type=F32)


def dot_full(a, b, contract):
    return lax.dot_general(
        a, b, (contract, ((), ())), precision=HIGHEST, preferred_element_type=F32
    )


def gram_kernel(scale, slab_ref, gram_ref, high_ref, low_ref):
    step = pl.program_id(0)
    cells, hours, kpis = slab_ref.shape
    block = slab_ref[...]
    upper = block[:, 0:8, :].reshape(cells * 8, kpis)
    half = cells // 2
    rest = jnp.concatenate([block[:half, 8:12, :], block[half:, 8:12, :]], axis=1)
    rows = jnp.concatenate([upper, rest.reshape(half * 8, kpis)], axis=0)
    high, low = split(rows)
    high_ref[0] = high
    low_ref[0] = low
    first = ((0,), (0,))
    cross = dot(high, low, first)
    part = dot(high, high, first) + dot(low, low, first) + (cross + cross.T)

    @pl.when(step == 0)
    def _():
        gram_ref[...] = part

    @pl.when(step > 0)
    def _():
        gram_ref[...] += part

    @pl.when(step == pl.num_programs(0) - 1)
    def _():
        gram_ref[...] = gram_ref[...] * scale


def slab_gram(slab, quarters, scale):
    cells, hours, kpis = slab.shape
    block = cells // quarters
    rows = block * hours
    return pl.pallas_call(
        functools.partial(gram_kernel, scale),
        grid=(quarters,),
        in_specs=[pl.BlockSpec((block, hours, kpis), lambda i: (i, 0, 0))],
        out_specs=[
            pl.BlockSpec((kpis, kpis), lambda i: (0, 0)),
            pl.BlockSpec((1, rows, kpis), lambda i: (i, 0, 0)),
            pl.BlockSpec((1, rows, kpis), lambda i: (i, 0, 0)),
        ],
        out_shape=[
            jax.ShapeDtypeStruct((kpis, kpis), F32),
            jax.ShapeDtypeStruct((quarters, rows, kpis), BF16),
            jax.ShapeDtypeStruct((quarters, rows, kpis), BF16),
        ],
        compiler_params=pltpu.CompilerParams(vmem_limit_bytes=40 * 2**20),
    )(slab)


def inverse_factor(gram):
    size = gram.shape[0]
    blocks = size // 8
    row_index = lax.broadcasted_iota(jnp.int32, (size, size), 0)
    column_index = lax.broadcasted_iota(jnp.int32, (size, size), 1)
    identity = jnp.where(row_index == column_index, 1.0, 0.0).astype(F32)
    whole = jnp.concatenate([gram, identity], axis=1)
    work = [whole[8 * b : 8 * b + 8, :] for b in range(blocks)]
    width = 2 * size
    sublane = lax.broadcasted_iota(jnp.int32, (8, width), 0)
    for panel in range(blocks):
        spread = {}
        for k in range(8):
            for b in range(panel, blocks):
                column = work[b][:, 8 * panel + k : 8 * panel + k + 1]
                spread[k, b] = jnp.broadcast_to(column, (8, width))
        for k in range(8):
            pivot_rows = [
                jnp.broadcast_to(spread[l, panel][k : k + 1, :], (8, width)) for l in range(k, 8)
            ]
            inverse = 1.0 / pivot_rows[0]
            pivot_work = jnp.broadcast_to(work[panel][k : k + 1, :], (8, width))
            for b in range(panel, blocks):
                factor = spread[k, b] * inverse
                if b == panel:
                    factor = jnp.where(sublane > k, factor, 0.0)
                for l in range(k + 1, 8):
                    spread[l, b] = spread[l, b] - factor * pivot_rows[l - k]
                work[b] = work[b] - factor * pivot_work
    whole = jnp.concatenate(work, axis=0)
    diagonal = jnp.sum(
        jnp.where(row_index == column_index, whole[:, :size], 0.0), axis=1, keepdims=True
    )
    return whole[:, size:] * lax.rsqrt(diagonal)


def orthonormalize(columns):
    for repeat in range(2):
        inner_gram = dot_full(columns, columns, ((0,), (0,)))
        inverse = inverse_factor(inner_gram)
        columns = dot_full(columns, inverse, ((1,), (1,)))
    return columns


def core_kernel(gram_ref, start_ref, high_ref, low_ref, subspace_ref, core_ref, high, low, sems):
    copies = [
        pltpu.make_async_copy(high_ref, high, sems.at[0]),
        pltpu.make_async_copy(low_ref, low, sems.at[1]),
    ]
    for copy in copies:
        copy.start()
    gram = gram_ref[...]
    subspace = start_ref[...]
    for repeat in range(POWER):
        subspace = orthonormalize(dot_full(gram, subspace, ((1,), (0,))))
    subspace_ref[...] = subspace
    quarters, rows, kpis = high.shape
    keep = subspace.shape[1]
    basis_high, basis_low = split(subspace)
    for copy in copies:
        copy.wait()
    plain = ((1,), (0,))

    def place(basis, q):
        parts = []
        if q:
            parts.append(jnp.zeros((kpis, keep * q), BF16))
        parts.append(basis)
        if q < quarters - 1:
            parts.append(jnp.zeros((kpis, keep * (quarters - 1 - q)), BF16))
        return jnp.concatenate(parts, axis=1)

    bases = [(place(basis_high, q), place(basis_low, q)) for q in range(quarters)]
    devices, piece, width = core_ref.shape
    group = piece // 3
    third = rows // 3
    for j in range(devices):
        for part in range(3):
            at = pl.ds(part * third + j * group, group)
            total = jnp.zeros((group, width), F32)
            for q in range(quarters):
                total += dot(high[q, at, :], bases[q][0], plain)
                total += dot(high[q, at, :], bases[q][1], plain)
                total += dot(low[q, at, :], bases[q][0], plain)
            core_ref[j, part * group : (part + 1) * group, :] = total


def subspace_and_core(gram, start, high, low, devices):
    quarters, rows, kpis = high.shape
    keep = start.shape[1]
    vmem = pl.BlockSpec(memory_space=pltpu.VMEM)
    hbm = pl.BlockSpec(memory_space=pl.ANY)
    return pl.pallas_call(
        core_kernel,
        in_specs=[vmem, vmem, hbm, hbm],
        out_specs=[vmem, vmem],
        out_shape=[
            jax.ShapeDtypeStruct((kpis, keep), F32),
            jax.ShapeDtypeStruct((devices, rows // devices, quarters * keep), F32),
        ],
        scratch_shapes=[
            pltpu.VMEM(high.shape, BF16),
            pltpu.VMEM(low.shape, BF16),
            pltpu.SemaphoreType.DMA((2,)),
        ],
        compiler_params=pltpu.CompilerParams(vmem_limit_bytes=40 * 2**20),
    )(gram, start, high, low)


def hour_kernel(hours, scale, core_ref, gram_ref):
    devices, piece, width = core_ref.shape
    group = piece // 3
    keep_first = lax.broadcasted_iota(jnp.int32, (8, width), 0) < hours - 8
    size = devices * 16
    total = jnp.zeros((size, size), F32)
    last = ((1,), (1,))
    for p in range(group // 8):
        for s in range(2):
            tiles = []
            for d in range(devices):
                tiles.append(core_ref[d, s * group + 8 * p : s * group + 8 * p + 8, :])
                rest = core_ref[d, 2 * group + 8 * p : 2 * group + 8 * p + 8, :]
                if s:
                    rest = pltpu.roll(rest, 4, 0)
                tiles.append(jnp.where(keep_first, rest, 0.0))
            high, low = split(jnp.concatenate(tiles, axis=0))
            cross = dot(high, low, last)
            total += dot(high, high, last) + dot(low, low, last) + (cross + cross.T)
    at = lax.broadcasted_iota(jnp.int32, (size, size), 0)
    to = lax.broadcasted_iota(jnp.int32, (size, size), 1)
    pick = jnp.where((at // 16) * hours + at % 16 == to, 1.0, 0.0)
    pick = jnp.where(at % 16 < hours, pick, 0.0).astype(F32)
    packed = dot_full(total, pick, ((1,), (0,))) * scale
    packed = packed.reshape(devices, 16, size)
    for copy in range(gram_ref.shape[0]):
        gram_ref[copy] = packed


def hour_gram_parts(core, hours, copies, scale):
    devices = core.shape[0]
    vmem = pl.BlockSpec(memory_space=pltpu.VMEM)
    return pl.pallas_call(
        functools.partial(hour_kernel, hours, scale),
        in_specs=[vmem],
        out_specs=vmem,
        out_shape=jax.ShapeDtypeStruct((copies, devices, 16, devices * 16), F32),
        compiler_params=pltpu.CompilerParams(vmem_limit_bytes=40 * 2**20),
    )(core)


def swap(values, axes):
    return lax.all_to_all(values, axes, 0, 0, tiled=True)


def far_sum(values):
    near_z = lax.axis_size("z_lo")
    copies = jnp.broadcast_to(values[None], (near_z,) + values.shape)
    return lax.psum(jnp.sum(swap(copies, "z_lo"), axis=0), "z_hi")


def local(slab, start):
    cell_count, hour_count, kpi_count = slab.shape
    keep_count = start.shape[1]
    hour_devices = lax.axis_size(HOUR)
    near_devices = lax.axis_size(NEAR)
    all_cells = cell_count * lax.axis_size(("z_hi", "z_lo", "y"))
    all_hours = hour_count * hour_devices
    quarters = 256 // keep_count

    partial_gram, high, low = slab_gram(slab, quarters, 1.0 / (all_cells * all_hours))
    pieces = partial_gram.reshape(near_devices, kpi_count // near_devices, kpi_count)
    piece = far_sum(jnp.sum(swap(pieces, NEAR), axis=0))
    pieces = swap(jnp.broadcast_to(piece[None], (near_devices,) + piece.shape), NEAR)
    kpi_gram = pieces.reshape(kpi_count, kpi_count)

    subspace, core = subspace_and_core(kpi_gram, start, high, low, hour_devices)
    core = swap(core, HOUR)
    y_devices = lax.axis_size("y")
    parts = hour_gram_parts(core, hour_count, y_devices, 1.0 / (all_cells * keep_count))
    parts = parts.reshape((near_devices,) + parts.shape[2:])
    rows = far_sum(jnp.sum(swap(parts, NEAR), axis=0))
    return subspace, rows[:hour_count, :all_hours]


def solution(mesh):
    fine = Mesh(
        mesh.devices.reshape(8, 4, 4, 4, 2), ("z_hi", "z_lo", "y", "x", "core")
    )
    return jax.shard_map(
        local,
        mesh=fine,
        in_specs=(P(("z_hi", "z_lo", "y"), HOUR, None), P()),
        out_specs=(P(), P(HOUR, None)),
        check_vma=False,
    )
```

```python
import functools

import jax
import jax.numpy as jnp
from jax import lax
from jax.experimental import pallas as pl
from jax.experimental.pallas import tpu as pltpu
from jax.sharding import Mesh, PartitionSpec as P

POWER = 2
F32 = jnp.float32
BF16 = jnp.bfloat16
HIGHEST = lax.Precision.HIGHEST
NEAR = ("y", "x", "core")
HOUR = ("x", "core")


def split(values):
    high = values.astype(BF16)
    low = (values - high.astype(F32)).astype(BF16)
    return high, low


def dot(a, b, contract):
    return lax.dot_general(a, b, (contract, ((), ())), preferred_element_type=F32)


def dot_full(a, b, contract):
    return lax.dot_general(
        a, b, (contract, ((), ())), precision=HIGHEST, preferred_element_type=F32
    )


def gram_kernel(scale, slab_ref, gram_ref, slab, sems):
    hours, cells, kpis = slab.shape
    count = sems.shape[0]
    step = hours // count
    copies = []
    for i in range(count):
        at = pl.ds(i * step, step)
        copies.append(pltpu.make_async_copy(slab_ref.at[at], slab.at[at], sems.at[i]))
        copies[-1].start()
    first = ((0,), (0,))
    even = jnp.zeros((kpis, kpis), F32)
    cross = jnp.zeros((kpis, kpis), F32)
    for i in range(count):
        at = pl.ds(i * step, step)
        copies[i].wait()
        high, low = split(slab[at].reshape(step * cells, kpis))
        cross += dot(high, low, first)
        even += dot(high, high, first) + dot(low, low, first)
    gram_ref[...] = (even + (cross + cross.T)) * scale


def slab_gram(slab, steps, scale):
    hours, cells, kpis = slab.shape
    return pl.pallas_call(
        functools.partial(gram_kernel, scale),
        in_specs=[pl.BlockSpec(memory_space=pl.ANY)],
        out_specs=pl.BlockSpec(memory_space=pltpu.VMEM),
        out_shape=jax.ShapeDtypeStruct((kpis, kpis), F32),
        scratch_shapes=[pltpu.VMEM(slab.shape, F32), pltpu.SemaphoreType.DMA((steps,))],
        compiler_params=pltpu.CompilerParams(vmem_limit_bytes=58 * 2**20),
    )(slab)


def inverse_factor(gram):
    size = gram.shape[0]
    blocks = size // 8
    width = 2 * size
    row_index = lax.broadcasted_iota(jnp.int32, (size, size), 0)
    column_index = lax.broadcasted_iota(jnp.int32, (size, size), 1)
    identity = jnp.where(row_index == column_index, 1.0, 0.0).astype(F32)
    whole = jnp.concatenate([gram, identity], axis=1)
    work = [whole[8 * b : 8 * b + 8, :] for b in range(blocks)]
    sublane = lax.broadcasted_iota(jnp.int32, (8, width), 0)

    def fill(values):
        return jnp.broadcast_to(values, (8, width))

    def spread(panel):
        first = 8 * panel
        return {
            (k, b): fill(work[b][:, first + k : first + k + 1])
            for k in range(8)
            for b in range(panel, blocks)
        }

    now = spread(0)
    for panel in range(blocks):
        later = spread(panel + 1) if panel + 1 < blocks else {}
        for k in range(8):
            inverse = 1.0 / fill(now[k, panel][k : k + 1, :])
            pivots = {m: fill(now[m, panel][k : k + 1, :]) for m in range(k + 1, 8)}
            if later:
                next_pivots = [fill(now[k, panel + 1][m : m + 1, :]) for m in range(8)]
            row = fill(work[panel][k : k + 1, :])
            for b in range(panel, blocks):
                factor = now[k, b] * inverse
                if b == panel:
                    factor = jnp.where(sublane > k, factor, 0.0)
                for m in range(k + 1, 8):
                    now[m, b] = now[m, b] - factor * pivots[m]
                if b > panel:
                    for m in range(8):
                        later[m, b] = later[m, b] - factor * next_pivots[m]
                work[b] = work[b] - factor * row
        now = later
    whole = jnp.concatenate(work, axis=0)
    diagonal = jnp.sum(
        jnp.where(row_index == column_index, whole[:, :size], 0.0), axis=1, keepdims=True
    )
    return whole[:, size:] * lax.rsqrt(diagonal)


def near_inverse_factor(gram):
    size = gram.shape[0]
    row_index = lax.broadcasted_iota(jnp.int32, (size, size), 0)
    column_index = lax.broadcasted_iota(jnp.int32, (size, size), 1)
    identity = jnp.where(row_index == column_index, 1.0, 0.0).astype(F32)
    weight = jnp.where(row_index > column_index, 1.0, 0.0).astype(F32) + 0.5 * identity
    apart = gram - identity

    def series(_):
        once = (weight * apart).astype(BF16)
        twice = weight * (apart - dot(once, once, ((1,), (1,))))
        rounded = twice.astype(BF16)
        return identity - twice + dot(rounded, rounded, ((1,), (0,)))

    return lax.cond(
        jnp.sum(apart * apart) < 2.5e-5, series, lambda _: inverse_factor(gram), 0
    )


def orthonormalize(columns):
    for factor in (inverse_factor, near_inverse_factor):
        inner_gram = dot_full(columns, columns, ((0,), (0,)))
        columns = dot_full(columns, factor(inner_gram), ((1,), (1,)))
    return columns


def core_kernel(gram_ref, start_ref, slab_ref, subspace_ref, core_ref):
    gram = gram_ref[...]
    subspace = start_ref[...].T
    for repeat in range(POWER):
        subspace = orthonormalize(dot_full(gram, subspace, ((1,), (0,))))
    subspace_ref[...] = subspace.T
    hours, cells, kpis = slab_ref.shape
    keep = subspace.shape[1]
    devices, _, group, width = core_ref.shape
    quarters = width // keep
    quarter = cells // quarters
    basis_high, basis_low = split(subspace)
    plain = ((1,), (0,))

    def place(basis, q):
        parts = []
        if q:
            parts.append(jnp.zeros((kpis, keep * q), BF16))
        parts.append(basis)
        if q < quarters - 1:
            parts.append(jnp.zeros((kpis, keep * (quarters - 1 - q)), BF16))
        return jnp.concatenate(parts, axis=1)

    bases = [(place(basis_high, q), place(basis_low, q)) for q in range(quarters)]
    batch = 4
    for h in range(0, hours, batch):
        total = jnp.zeros((batch * quarter, width), F32)
        for q in range(quarters):
            at = pl.ds(q * quarter, quarter)
            top, rest = split(slab_ref[h : h + batch, at, :].reshape(batch * quarter, kpis))
            total += dot(top, bases[q][0], plain)
            total += dot(top, bases[q][1], plain)
            total += dot(rest, bases[q][0], plain)
        for i in range(batch):
            for j in range(devices):
                at = i * quarter + j * group
                core_ref[j, h + i] = total[at : at + group]


def subspace_and_core(gram, start, slab, devices):
    hours, cells, kpis = slab.shape
    keep = start.shape[0]
    width = 256
    group = cells * keep // width // devices
    vmem = pl.BlockSpec(memory_space=pltpu.VMEM)
    return pl.pallas_call(
        core_kernel,
        in_specs=[vmem] * 3,
        out_specs=[vmem, vmem],
        out_shape=[
            jax.ShapeDtypeStruct((keep, kpis), F32),
            jax.ShapeDtypeStruct((devices, hours, group, width), F32),
        ],
        compiler_params=pltpu.CompilerParams(vmem_limit_bytes=40 * 2**20),
    )(gram, start, slab)


def hour_kernel(hours, scale, core_ref, gram_ref, halves):
    group = 8
    rows, width = core_ref.shape
    lanes = halves.shape[2]
    for part in range(width // lanes):
        halves[part] = core_ref[:, part * lanes : (part + 1) * lanes]
    all_hours = rows // group
    devices = all_hours // hours
    total = jnp.zeros((all_hours, all_hours), F32)
    last = ((1,), (1,))
    for i in range(group):
        parts = [
            halves[part, pl.ds(i, all_hours, stride=group), :] for part in range(width // lanes)
        ]
        high, low = split(jnp.concatenate(parts, axis=1))
        cross = dot(high, low, last)
        total += dot(high, high, last) + dot(low, low, last) + (cross + cross.T)
    total = total * scale
    for d in range(devices):
        block = total[d * hours : (d + 1) * hours, :]
        for copy in range(gram_ref.shape[0] // devices):
            gram_ref[copy * devices + d] = block


def hour_gram_parts(core, hours, copies, scale):
    group, width = core.shape[2:]
    all_hours = core.shape[0] * core.shape[1]
    vmem = pl.BlockSpec(memory_space=pltpu.VMEM)
    return pl.pallas_call(
        functools.partial(hour_kernel, hours, scale),
        in_specs=[vmem],
        out_specs=vmem,
        out_shape=jax.ShapeDtypeStruct((copies * core.shape[0], hours, all_hours), F32),
        scratch_shapes=[pltpu.VMEM((width // 128, all_hours * group, 128), F32)],
        compiler_params=pltpu.CompilerParams(vmem_limit_bytes=40 * 2**20),
    )(core.reshape(all_hours * group, width))


def swap(values, axes):
    return lax.all_to_all(values, axes, 0, 0, tiled=True)


def far_sum(values):
    return lax.psum(lax.optimization_barrier(lax.psum(values, "z_lo")), "z_hi")


def local(slab, start):
    cell_count, hour_count, kpi_count = slab.shape
    keep_count = start.shape[1]
    hour_devices = lax.axis_size(HOUR)
    near_devices = lax.axis_size(NEAR)
    all_cells = cell_count * lax.axis_size(("z_hi", "z_lo", "y"))
    all_hours = hour_count * hour_devices
    y_devices = lax.axis_size("y")

    slab = jnp.transpose(slab, (1, 0, 2))
    partial_gram = slab_gram(slab, 2, 1.0 / (all_cells * all_hours))
    pieces = partial_gram.reshape(near_devices, kpi_count // near_devices, kpi_count)
    piece = far_sum(jnp.sum(swap(pieces, NEAR), axis=0))
    pieces = swap(jnp.broadcast_to(piece[None], (near_devices,) + piece.shape), NEAR)
    kpi_gram = pieces.reshape(kpi_count, kpi_count)

    subspace, core = subspace_and_core(kpi_gram, start.T, slab, hour_devices)
    core = swap(core, HOUR)
    parts = hour_gram_parts(core, hour_count, y_devices, 1.0 / (all_cells * keep_count))
    hour_gram = far_sum(jnp.sum(swap(parts, NEAR), axis=0))
    return subspace.T, hour_gram


def solution(mesh):
    fine = Mesh(
        mesh.devices.reshape(8, 4, 4, 4, 2), ("z_hi", "z_lo", "y", "x", "core")
    )
    return jax.shard_map(
        local,
        mesh=fine,
        in_specs=(P(("z_hi", "z_lo", "y"), HOUR, None), P()),
        out_specs=(P(), P(HOUR, None)),
        check_vma=False,
    )
```

```python
import functools

import jax
import jax.numpy as jnp
from jax import lax
from jax.experimental import pallas as pl
from jax.experimental.pallas import tpu as pltpu
from jax.sharding import Mesh, PartitionSpec as P

POWER = 2
F32 = jnp.float32
BF16 = jnp.bfloat16
HIGHEST = lax.Precision.HIGHEST
NEAR = ("y", "x", "core")
HOUR = ("x", "core")


def split(values):
    high = values.astype(BF16)
    low = (values - high.astype(F32)).astype(BF16)
    return high, low


def dot(a, b, contract):
    return lax.dot_general(a, b, (contract, ((), ())), preferred_element_type=F32)


def dot_full(a, b, contract):
    return lax.dot_general(
        a, b, (contract, ((), ())), precision=HIGHEST, preferred_element_type=F32
    )


def gram_kernel(scale, slab_ref, gram_ref, slab, sems):
    hours, cells, kpis = slab.shape
    count = sems.shape[0]
    step = hours // count
    copies = []
    for i in range(count):
        at = pl.ds(i * step, step)
        copies.append(pltpu.make_async_copy(slab_ref.at[at], slab.at[at], sems.at[i]))
        copies[-1].start()
    first = ((0,), (0,))
    even = jnp.zeros((kpis, kpis), F32)
    cross = jnp.zeros((kpis, kpis), F32)
    for i in range(count):
        at = pl.ds(i * step, step)
        copies[i].wait()
        high, low = split(slab[at].reshape(step * cells, kpis))
        cross += dot(high, low, first)
        even += dot(high, high, first) + dot(low, low, first)
    gram_ref[...] = (even + (cross + cross.T)) * scale


def slab_gram(slab, steps, scale):
    hours, cells, kpis = slab.shape
    return pl.pallas_call(
        functools.partial(gram_kernel, scale),
        in_specs=[pl.BlockSpec(memory_space=pl.ANY)],
        out_specs=pl.BlockSpec(memory_space=pltpu.VMEM),
        out_shape=jax.ShapeDtypeStruct((kpis, kpis), F32),
        scratch_shapes=[pltpu.VMEM(slab.shape, F32), pltpu.SemaphoreType.DMA((steps,))],
        compiler_params=pltpu.CompilerParams(vmem_limit_bytes=58 * 2**20),
    )(slab)


def inverse_factor(gram):
    size = gram.shape[0]
    blocks = size // 8
    width = 2 * size
    row_index = lax.broadcasted_iota(jnp.int32, (size, size), 0)
    column_index = lax.broadcasted_iota(jnp.int32, (size, size), 1)
    identity = jnp.where(row_index == column_index, 1.0, 0.0).astype(F32)
    whole = jnp.concatenate([gram, identity], axis=1)
    work = [whole[8 * b : 8 * b + 8, :] for b in range(blocks)]
    sublane = lax.broadcasted_iota(jnp.int32, (8, width), 0)

    def fill(values):
        return jnp.broadcast_to(values, (8, width))

    def spread(panel):
        first = 8 * panel
        return {
            (k, b): fill(work[b][:, first + k : first + k + 1])
            for k in range(8)
            for b in range(panel, blocks)
        }

    now = spread(0)
    for panel in range(blocks):
        later = spread(panel + 1) if panel + 1 < blocks else {}
        for k in range(8):
            inverse = 1.0 / fill(now[k, panel][k : k + 1, :])
            pivots = {m: fill(now[m, panel][k : k + 1, :]) for m in range(k + 1, 8)}
            if later:
                next_pivots = [fill(now[k, panel + 1][m : m + 1, :]) for m in range(8)]
            row = fill(work[panel][k : k + 1, :])
            for b in range(panel, blocks):
                factor = now[k, b] * inverse
                if b == panel:
                    factor = jnp.where(sublane > k, factor, 0.0)
                for m in range(k + 1, 8):
                    now[m, b] = now[m, b] - factor * pivots[m]
                if b > panel:
                    for m in range(8):
                        later[m, b] = later[m, b] - factor * next_pivots[m]
                work[b] = work[b] - factor * row
        now = later
    whole = jnp.concatenate(work, axis=0)
    diagonal = jnp.sum(
        jnp.where(row_index == column_index, whole[:, :size], 0.0), axis=1, keepdims=True
    )
    return whole[:, size:] * lax.rsqrt(diagonal)


def near_inverse_factor(gram):
    size = gram.shape[0]
    row_index = lax.broadcasted_iota(jnp.int32, (size, size), 0)
    column_index = lax.broadcasted_iota(jnp.int32, (size, size), 1)
    identity = jnp.where(row_index == column_index, 1.0, 0.0).astype(F32)
    weight = jnp.where(row_index > column_index, 1.0, 0.0).astype(F32) + 0.5 * identity
    apart = gram - identity

    def series(_):
        once = (weight * apart).astype(BF16)
        twice = weight * (apart - dot(once, once, ((1,), (1,))))
        rounded = twice.astype(BF16)
        return identity - twice + dot(rounded, rounded, ((1,), (0,)))

    return lax.cond(
        jnp.sum(apart * apart) < 2.5e-5, series, lambda _: inverse_factor(gram), 0
    )


def orthonormalize(columns):
    for factor in (inverse_factor, near_inverse_factor):
        inner_gram = dot_full(columns, columns, ((0,), (0,)))
        columns = dot_full(columns, factor(inner_gram), ((1,), (1,)))
    return columns


def core_kernel(gram_ref, start_ref, slab_ref, subspace_ref, core_ref, slab, sem):
    copy = pltpu.make_async_copy(slab_ref, slab, sem)
    copy.start()
    gram = gram_ref[...]
    subspace = start_ref[...].T
    for repeat in range(POWER):
        subspace = orthonormalize(dot_full(gram, subspace, ((1,), (0,))))
    subspace_ref[...] = subspace.T
    hours, cells, kpis = slab.shape
    keep = subspace.shape[1]
    devices, _, group, width = core_ref.shape
    quarters = width // keep
    quarter = cells // quarters
    basis_high, basis_low = split(subspace)
    copy.wait()
    plain = ((1,), (0,))

    def place(basis, q):
        parts = []
        if q:
            parts.append(jnp.zeros((kpis, keep * q), BF16))
        parts.append(basis)
        if q < quarters - 1:
            parts.append(jnp.zeros((kpis, keep * (quarters - 1 - q)), BF16))
        return jnp.concatenate(parts, axis=1)

    bases = [(place(basis_high, q), place(basis_low, q)) for q in range(quarters)]
    batch = 4
    for h in range(0, hours, batch):
        total = jnp.zeros((batch * quarter, width), F32)
        for q in range(quarters):
            at = pl.ds(q * quarter, quarter)
            top, rest = split(slab[h : h + batch, at, :].reshape(batch * quarter, kpis))
            total += dot(top, bases[q][0], plain)
            total += dot(top, bases[q][1], plain)
            total += dot(rest, bases[q][0], plain)
        for i in range(batch):
            for j in range(devices):
                at = i * quarter + j * group
                core_ref[j, h + i] = total[at : at + group]


def subspace_and_core(gram, start, slab, devices):
    hours, cells, kpis = slab.shape
    keep = start.shape[0]
    width = 256
    group = cells * keep // width // devices
    vmem = pl.BlockSpec(memory_space=pltpu.VMEM)
    return pl.pallas_call(
        core_kernel,
        in_specs=[vmem, vmem, pl.BlockSpec(memory_space=pl.ANY)],
        out_specs=[vmem, vmem],
        out_shape=[
            jax.ShapeDtypeStruct((keep, kpis), F32),
            jax.ShapeDtypeStruct((devices, hours, group, width), F32),
        ],
        scratch_shapes=[pltpu.VMEM(slab.shape, F32), pltpu.SemaphoreType.DMA],
        compiler_params=pltpu.CompilerParams(vmem_limit_bytes=56 * 2**20),
    )(gram, start, slab)


def hour_kernel(hours, scale, core_ref, gram_ref, halves):
    group = 8
    rows, width = core_ref.shape
    lanes = halves.shape[2]
    for part in range(width // lanes):
        halves[part] = core_ref[:, part * lanes : (part + 1) * lanes]
    all_hours = rows // group
    devices = all_hours // hours
    total = jnp.zeros((all_hours, all_hours), F32)
    last = ((1,), (1,))
    for i in range(group):
        parts = [
            halves[part, pl.ds(i, all_hours, stride=group), :] for part in range(width // lanes)
        ]
        high, low = split(jnp.concatenate(parts, axis=1))
        cross = dot(high, low, last)
        total += dot(high, high, last) + dot(low, low, last) + (cross + cross.T)
    total = total * scale
    for d in range(devices):
        gram_ref[d] = total[d * hours : (d + 1) * hours, :]


def hour_gram_parts(core, hours, scale):
    group, width = core.shape[2:]
    all_hours = core.shape[0] * core.shape[1]
    vmem = pl.BlockSpec(memory_space=pltpu.VMEM)
    return pl.pallas_call(
        functools.partial(hour_kernel, hours, scale),
        in_specs=[vmem],
        out_specs=vmem,
        out_shape=jax.ShapeDtypeStruct((core.shape[0], hours, all_hours), F32),
        scratch_shapes=[pltpu.VMEM((width // 128, all_hours * group, 128), F32)],
        compiler_params=pltpu.CompilerParams(vmem_limit_bytes=40 * 2**20),
    )(core.reshape(all_hours * group, width))


def swap(values, axes):
    return lax.all_to_all(values, axes, 0, 0, tiled=True)


def spread_out(values, axes):
    count = lax.axis_size(axes)
    return swap(jnp.broadcast_to(values[None], (count,) + values.shape), axes)


def local(slab, start):
    cell_count, hour_count, kpi_count = slab.shape
    keep_count = start.shape[1]
    hour_devices = lax.axis_size(HOUR)
    near_devices = lax.axis_size(NEAR)
    all_cells = cell_count * lax.axis_size(("z_hi", "z_lo", "y"))
    all_hours = hour_count * hour_devices

    slab = jnp.transpose(slab, (1, 0, 2))
    partial_gram = slab_gram(slab, 2, 1.0 / (all_cells * all_hours))
    pieces = partial_gram.reshape(near_devices, kpi_count // near_devices, kpi_count)
    piece = lax.psum(jnp.sum(swap(pieces, NEAR), axis=0), "z_lo")
    piece = lax.psum(lax.optimization_barrier(piece), "z_hi")
    kpi_gram = spread_out(piece, NEAR).reshape(kpi_count, kpi_count)

    subspace, core = subspace_and_core(kpi_gram, start.T, slab, hour_devices)
    core = swap(core, HOUR)
    parts = hour_gram_parts(core, hour_count, 1.0 / (all_cells * keep_count))
    rows = jnp.sum(swap(parts, HOUR), axis=0)
    rows = jnp.sum(spread_out(rows, ("z_lo", "y")), axis=0)
    hour_gram = lax.psum(rows, "z_hi")
    return subspace.T, hour_gram


def solution(mesh):
    fine = Mesh(
        mesh.devices.reshape(8, 4, 4, 4, 2), ("z_hi", "z_lo", "y", "x", "core")
    )
    return jax.shard_map(
        local,
        mesh=fine,
        in_specs=(P(("z_hi", "z_lo", "y"), HOUR, None), P()),
        out_specs=(P(), P(HOUR, None)),
        check_vma=False,
    )
```

```python
import functools

import jax
import jax.numpy as jnp
from jax import lax
from jax.experimental import pallas as pl
from jax.experimental.pallas import tpu as pltpu
from jax.sharding import Mesh, PartitionSpec as P

POWER = 2
F32 = jnp.float32
BF16 = jnp.bfloat16
HIGHEST = lax.Precision.HIGHEST
NEAR = ("y", "x", "core")
HOUR = ("x", "core")


def split(values):
    high = values.astype(BF16)
    low = (values - high.astype(F32)).astype(BF16)
    return high, low


def dot(a, b, contract):
    return lax.dot_general(a, b, (contract, ((), ())), preferred_element_type=F32)


def dot_full(a, b, contract):
    return lax.dot_general(
        a, b, (contract, ((), ())), precision=HIGHEST, preferred_element_type=F32
    )


def gram_kernel(scale, slab_ref, gram_ref, slab, sems):
    hours, cells, kpis = slab.shape
    count = sems.shape[0]
    step = hours // count
    copies = []
    for i in range(count):
        at = pl.ds(i * step, step)
        copies.append(pltpu.make_async_copy(slab_ref.at[at], slab.at[at], sems.at[i]))
        copies[-1].start()
    first = ((0,), (0,))
    even = jnp.zeros((kpis, kpis), F32)
    cross = jnp.zeros((kpis, kpis), F32)
    for i in range(count):
        at = pl.ds(i * step, step)
        copies[i].wait()
        high, low = split(slab[at].reshape(step * cells, kpis))
        cross += dot(high, low, first)
        even += dot(high, high, first) + dot(low, low, first)
    gram_ref[...] = (even + (cross + cross.T)) * scale


def slab_gram(slab, steps, scale):
    hours, cells, kpis = slab.shape
    return pl.pallas_call(
        functools.partial(gram_kernel, scale),
        in_specs=[pl.BlockSpec(memory_space=pl.ANY)],
        out_specs=[pl.BlockSpec(memory_space=pltpu.VMEM)] * 2,
        out_shape=[pltpu.VMEM((kpis, kpis), F32), pltpu.VMEM(slab.shape, F32)],
        scratch_shapes=[pltpu.SemaphoreType.DMA((steps,))],
        compiler_params=pltpu.CompilerParams(vmem_limit_bytes=58 * 2**20),
    )(slab)


def inverse_factor(gram):
    size = gram.shape[0]
    blocks = size // 8
    width = 2 * size
    row_index = lax.broadcasted_iota(jnp.int32, (size, size), 0)
    column_index = lax.broadcasted_iota(jnp.int32, (size, size), 1)
    identity = jnp.where(row_index == column_index, 1.0, 0.0).astype(F32)
    whole = jnp.concatenate([gram, identity], axis=1)
    work = [whole[8 * b : 8 * b + 8, :] for b in range(blocks)]
    sublane = lax.broadcasted_iota(jnp.int32, (8, width), 0)

    def fill(values):
        return jnp.broadcast_to(values, (8, width))

    def spread(panel):
        first = 8 * panel
        return {
            (k, b): fill(work[b][:, first + k : first + k + 1])
            for k in range(8)
            for b in range(panel, blocks)
        }

    now = spread(0)
    for panel in range(blocks):
        later = spread(panel + 1) if panel + 1 < blocks else {}
        for k in range(8):
            inverse = 1.0 / fill(now[k, panel][k : k + 1, :])
            pivots = {m: fill(now[m, panel][k : k + 1, :]) for m in range(k + 1, 8)}
            if later:
                next_pivots = [fill(now[k, panel + 1][m : m + 1, :]) for m in range(8)]
            row = fill(work[panel][k : k + 1, :])
            for b in range(panel, blocks):
                factor = now[k, b] * inverse
                if b == panel:
                    factor = jnp.where(sublane > k, factor, 0.0)
                for m in range(k + 1, 8):
                    now[m, b] = now[m, b] - factor * pivots[m]
                if b > panel:
                    for m in range(8):
                        later[m, b] = later[m, b] - factor * next_pivots[m]
                work[b] = work[b] - factor * row
        now = later
    whole = jnp.concatenate(work, axis=0)
    diagonal = jnp.sum(
        jnp.where(row_index == column_index, whole[:, :size], 0.0), axis=1, keepdims=True
    )
    return whole[:, size:] * lax.rsqrt(diagonal)


def near_inverse_factor(gram):
    size = gram.shape[0]
    row_index = lax.broadcasted_iota(jnp.int32, (size, size), 0)
    column_index = lax.broadcasted_iota(jnp.int32, (size, size), 1)
    identity = jnp.where(row_index == column_index, 1.0, 0.0).astype(F32)
    weight = jnp.where(row_index > column_index, 1.0, 0.0).astype(F32) + 0.5 * identity
    apart = gram - identity

    def series(_):
        once = (weight * apart).astype(BF16)
        twice = weight * (apart - dot(once, once, ((1,), (1,))))
        rounded = twice.astype(BF16)
        return identity - twice + dot(rounded, rounded, ((1,), (0,)))

    return lax.cond(
        jnp.sum(apart * apart) < 2.5e-5, series, lambda _: inverse_factor(gram), 0
    )


def orthonormalize(columns):
    for factor in (inverse_factor, near_inverse_factor):
        inner_gram = dot_full(columns, columns, ((0,), (0,)))
        columns = dot_full(columns, factor(inner_gram), ((1,), (1,)))
    return columns


def core_kernel(gram_ref, start_ref, slab_ref, subspace_ref, core_ref):
    gram = gram_ref[...]
    subspace = start_ref[...].T
    for repeat in range(POWER):
        subspace = orthonormalize(dot_full(gram, subspace, ((1,), (0,))))
    subspace_ref[...] = subspace.T
    hours, cells, kpis = slab_ref.shape
    keep = subspace.shape[1]
    devices, _, group, width = core_ref.shape
    quarters = width // keep
    quarter = cells // quarters
    basis_high, basis_low = split(subspace)
    plain = ((1,), (0,))

    def place(basis, q):
        parts = []
        if q:
            parts.append(jnp.zeros((kpis, keep * q), BF16))
        parts.append(basis)
        if q < quarters - 1:
            parts.append(jnp.zeros((kpis, keep * (quarters - 1 - q)), BF16))
        return jnp.concatenate(parts, axis=1)

    bases = [(place(basis_high, q), place(basis_low, q)) for q in range(quarters)]
    batch = 4
    for h in range(0, hours, batch):
        total = jnp.zeros((batch * quarter, width), F32)
        for q in range(quarters):
            at = pl.ds(q * quarter, quarter)
            top, rest = split(slab_ref[h : h + batch, at, :].reshape(batch * quarter, kpis))
            total += dot(top, bases[q][0], plain)
            total += dot(top, bases[q][1], plain)
            total += dot(rest, bases[q][0], plain)
        for i in range(batch):
            for j in range(devices):
                at = i * quarter + j * group
                core_ref[j, h + i] = total[at : at + group]


def subspace_and_core(gram, start, slab, devices):
    hours, cells, kpis = slab.shape
    keep = start.shape[0]
    width = 256
    group = cells * keep // width // devices
    vmem = pl.BlockSpec(memory_space=pltpu.VMEM)
    return pl.pallas_call(
        core_kernel,
        in_specs=[vmem] * 3,
        out_specs=[vmem, vmem],
        out_shape=[
            jax.ShapeDtypeStruct((keep, kpis), F32),
            pltpu.VMEM((devices, hours, group, width), F32),
        ],
        compiler_params=pltpu.CompilerParams(vmem_limit_bytes=40 * 2**20),
    )(gram, start, slab)


def hour_kernel(hours, scale, core_ref, gram_ref, halves):
    group = 8
    rows, width = core_ref.shape
    lanes = halves.shape[2]
    for part in range(width // lanes):
        halves[part] = core_ref[:, part * lanes : (part + 1) * lanes]
    all_hours = rows // group
    devices = all_hours // hours
    total = jnp.zeros((all_hours, all_hours), F32)
    last = ((1,), (1,))
    for i in range(group):
        parts = [
            halves[part, pl.ds(i, all_hours, stride=group), :] for part in range(width // lanes)
        ]
        high, low = split(jnp.concatenate(parts, axis=1))
        cross = dot(high, low, last)
        total += dot(high, high, last) + dot(low, low, last) + (cross + cross.T)
    total = total * scale
    for d in range(devices):
        gram_ref[d] = total[d * hours : (d + 1) * hours, :]


def hour_gram_parts(core, hours, scale):
    group, width = core.shape[2:]
    all_hours = core.shape[0] * core.shape[1]
    vmem = pl.BlockSpec(memory_space=pltpu.VMEM)
    return pl.pallas_call(
        functools.partial(hour_kernel, hours, scale),
        in_specs=[vmem],
        out_specs=vmem,
        out_shape=jax.ShapeDtypeStruct((core.shape[0], hours, all_hours), F32),
        scratch_shapes=[pltpu.VMEM((width // 128, all_hours * group, 128), F32)],
        compiler_params=pltpu.CompilerParams(vmem_limit_bytes=40 * 2**20),
    )(core.reshape(all_hours * group, width))


def swap(values, axes):
    return lax.all_to_all(values, axes, 0, 0, tiled=True)


def spread_out(values, axes):
    count = lax.axis_size(axes)
    return swap(jnp.broadcast_to(values[None], (count,) + values.shape), axes)


def local(slab, start):
    cell_count, hour_count, kpi_count = slab.shape
    keep_count = start.shape[1]
    hour_devices = lax.axis_size(HOUR)
    near_devices = lax.axis_size(NEAR)
    all_cells = cell_count * lax.axis_size(("z_hi", "z_lo", "y"))
    all_hours = hour_count * hour_devices

    slab = jnp.transpose(slab, (1, 0, 2))
    partial_gram, slab = slab_gram(slab, 2, 1.0 / (all_cells * all_hours))
    pieces = partial_gram.reshape(near_devices, kpi_count // near_devices, kpi_count)
    piece = lax.psum(jnp.sum(swap(pieces, NEAR), axis=0), "z_lo")
    piece = lax.psum(lax.optimization_barrier(piece), "z_hi")
    kpi_gram = spread_out(piece, NEAR).reshape(kpi_count, kpi_count)

    subspace, core = subspace_and_core(kpi_gram, start.T, slab, hour_devices)
    core = swap(core, HOUR)
    parts = hour_gram_parts(core, hour_count, 1.0 / (all_cells * keep_count))
    rows = jnp.sum(swap(parts, HOUR), axis=0)
    rows = jnp.sum(spread_out(rows, ("z_lo", "y")), axis=0)
    hour_gram = lax.psum(rows, "z_hi")
    return subspace.T, hour_gram


def solution(mesh):
    fine = Mesh(
        mesh.devices.reshape(8, 4, 4, 4, 2), ("z_hi", "z_lo", "y", "x", "core")
    )
    return jax.shard_map(
        local,
        mesh=fine,
        in_specs=(P(("z_hi", "z_lo", "y"), HOUR, None), P()),
        out_specs=(P(), P(HOUR, None)),
        check_vma=False,
    )
```

```python
import functools

import jax
import jax.numpy as jnp
from jax import lax
from jax.experimental import pallas as pl
from jax.experimental.pallas import tpu as pltpu
from jax.sharding import Mesh, PartitionSpec as P

POWER = 2
F32 = jnp.float32
BF16 = jnp.bfloat16
HIGHEST = lax.Precision.HIGHEST
NEAR = ("y", "x", "core")
HOUR = ("x", "core")


def split(values):
    high = values.astype(BF16)
    low = (values - high.astype(F32)).astype(BF16)
    return high, low


def dot(a, b, contract):
    return lax.dot_general(a, b, (contract, ((), ())), preferred_element_type=F32)


def dot_full(a, b, contract):
    return lax.dot_general(
        a, b, (contract, ((), ())), precision=HIGHEST, preferred_element_type=F32
    )


def gram_kernel(scale, slab_ref, gram_ref, slab, sems):
    hours, cells, kpis = slab.shape
    count = sems.shape[0]
    step = hours // count
    copies = []
    for i in range(count):
        at = pl.ds(i * step, step)
        copies.append(pltpu.make_async_copy(slab_ref.at[at], slab.at[at], sems.at[i]))
        copies[-1].start()
    first = ((0,), (0,))
    even = jnp.zeros((kpis, kpis), F32)
    cross = jnp.zeros((kpis, kpis), F32)
    for i in range(count):
        at = pl.ds(i * step, step)
        copies[i].wait()
        high, low = split(slab[at].reshape(step * cells, kpis))
        cross += dot(high, low, first)
        even += dot(high, high, first) + dot(low, low, first)
    gram_ref[...] = (even + (cross + cross.T)) * scale


def slab_gram(slab, steps, scale):
    hours, cells, kpis = slab.shape
    return pl.pallas_call(
        functools.partial(gram_kernel, scale),
        in_specs=[pl.BlockSpec(memory_space=pl.ANY)],
        out_specs=[pl.BlockSpec(memory_space=pltpu.VMEM)] * 2,
        out_shape=[pltpu.VMEM((kpis, kpis), F32), pltpu.VMEM(slab.shape, F32)],
        scratch_shapes=[pltpu.SemaphoreType.DMA((steps,))],
        compiler_params=pltpu.CompilerParams(vmem_limit_bytes=58 * 2**20),
    )(slab)


def inverse_factor(gram):
    size = gram.shape[0]
    blocks = size // 8
    width = 2 * size
    row_index = lax.broadcasted_iota(jnp.int32, (size, size), 0)
    column_index = lax.broadcasted_iota(jnp.int32, (size, size), 1)
    identity = jnp.where(row_index == column_index, 1.0, 0.0).astype(F32)
    whole = jnp.concatenate([gram, identity], axis=1)
    work = [whole[8 * b : 8 * b + 8, :] for b in range(blocks)]
    sublane = lax.broadcasted_iota(jnp.int32, (8, width), 0)

    def fill(values):
        return jnp.broadcast_to(values, (8, width))

    def spread(panel):
        first = 8 * panel
        return {
            (k, b): fill(work[b][:, first + k : first + k + 1])
            for k in range(8)
            for b in range(panel, blocks)
        }

    now = spread(0)
    for panel in range(blocks):
        later = spread(panel + 1) if panel + 1 < blocks else {}
        for k in range(8):
            inverse = 1.0 / fill(now[k, panel][k : k + 1, :])
            pivots = {m: fill(now[m, panel][k : k + 1, :]) for m in range(k + 1, 8)}
            if later:
                next_pivots = [fill(now[k, panel + 1][m : m + 1, :]) for m in range(8)]
            row = fill(work[panel][k : k + 1, :])
            for b in range(panel, blocks):
                factor = now[k, b] * inverse
                if b == panel:
                    factor = jnp.where(sublane > k, factor, 0.0)
                for m in range(k + 1, 8):
                    now[m, b] = now[m, b] - factor * pivots[m]
                if b > panel:
                    for m in range(8):
                        later[m, b] = later[m, b] - factor * next_pivots[m]
                work[b] = work[b] - factor * row
        now = later
    whole = jnp.concatenate(work, axis=0)
    diagonal = jnp.sum(
        jnp.where(row_index == column_index, whole[:, :size], 0.0), axis=1, keepdims=True
    )
    return whole[:, size:] * lax.rsqrt(diagonal)


def near_inverse_factor(gram):
    size = gram.shape[0]
    row_index = lax.broadcasted_iota(jnp.int32, (size, size), 0)
    column_index = lax.broadcasted_iota(jnp.int32, (size, size), 1)
    identity = jnp.where(row_index == column_index, 1.0, 0.0).astype(F32)
    weight = jnp.where(row_index > column_index, 1.0, 0.0).astype(F32) + 0.5 * identity
    apart = gram - identity

    def series(_):
        once = (weight * apart).astype(BF16)
        twice = weight * (apart - dot(once, once, ((1,), (1,))))
        rounded = twice.astype(BF16)
        return identity - twice + dot(rounded, rounded, ((1,), (0,)))

    return lax.cond(
        jnp.sum(apart * apart) < 2.5e-5, series, lambda _: inverse_factor(gram), 0
    )


def orthonormalize(rows):
    for factor in (inverse_factor, near_inverse_factor):
        inner_gram = dot_full(rows, rows, ((1,), (1,)))
        rows = dot_full(factor(inner_gram), rows, ((1,), (0,)))
    return rows


def core_kernel(gram_ref, start_ref, slab_ref, subspace_ref, core_ref):
    gram = gram_ref[...]
    subspace = start_ref[...]
    for repeat in range(POWER):
        subspace = orthonormalize(dot_full(subspace, gram, ((1,), (0,))))
    subspace_ref[...] = subspace
    hours, cells, kpis = slab_ref.shape
    keep = subspace.shape[0]
    devices, _, group, width = core_ref.shape
    quarters = width // keep
    quarter = cells // quarters
    basis_high, basis_low = split(subspace)
    last = ((1,), (1,))

    def place(basis, q):
        parts = []
        if q:
            parts.append(jnp.zeros((keep * q, kpis), BF16))
        parts.append(basis)
        if q < quarters - 1:
            parts.append(jnp.zeros((keep * (quarters - 1 - q), kpis), BF16))
        return jnp.concatenate(parts, axis=0)

    bases = [(place(basis_high, q), place(basis_low, q)) for q in range(quarters)]
    batch = 4
    for h in range(0, hours, batch):
        total = jnp.zeros((batch * quarter, width), F32)
        for q in range(quarters):
            at = pl.ds(q * quarter, quarter)
            top, rest = split(slab_ref[h : h + batch, at, :].reshape(batch * quarter, kpis))
            total += dot(top, bases[q][0], last)
            total += dot(top, bases[q][1], last)
            total += dot(rest, bases[q][0], last)
        for i in range(batch):
            for j in range(devices):
                at = i * quarter + j * group
                core_ref[j, h + i] = total[at : at + group]


def subspace_and_core(gram, start, slab, devices):
    hours, cells, kpis = slab.shape
    keep = start.shape[0]
    width = 256
    group = cells * keep // width // devices
    vmem = pl.BlockSpec(memory_space=pltpu.VMEM)
    return pl.pallas_call(
        core_kernel,
        in_specs=[vmem] * 3,
        out_specs=[vmem, vmem],
        out_shape=[
            jax.ShapeDtypeStruct((keep, kpis), F32),
            pltpu.VMEM((devices, hours, group, width), F32),
        ],
        compiler_params=pltpu.CompilerParams(vmem_limit_bytes=40 * 2**20),
    )(gram, start, slab)


def hour_kernel(hours, scale, core_ref, gram_ref, halves):
    group = 8
    rows, width = core_ref.shape
    lanes = halves.shape[2]
    for part in range(width // lanes):
        halves[part] = core_ref[:, part * lanes : (part + 1) * lanes]
    all_hours = rows // group
    devices = all_hours // hours
    total = jnp.zeros((all_hours, all_hours), F32)
    last = ((1,), (1,))
    for i in range(group):
        parts = [
            halves[part, pl.ds(i, all_hours, stride=group), :] for part in range(width // lanes)
        ]
        high, low = split(jnp.concatenate(parts, axis=1))
        cross = dot(high, low, last)
        total += dot(high, high, last) + dot(low, low, last) + (cross + cross.T)
    total = total * scale
    for d in range(devices):
        gram_ref[d] = total[d * hours : (d + 1) * hours, :]


def hour_gram_parts(core, hours, scale):
    group, width = core.shape[2:]
    all_hours = core.shape[0] * core.shape[1]
    vmem = pl.BlockSpec(memory_space=pltpu.VMEM)
    return pl.pallas_call(
        functools.partial(hour_kernel, hours, scale),
        in_specs=[vmem],
        out_specs=vmem,
        out_shape=jax.ShapeDtypeStruct((core.shape[0], hours, all_hours), F32),
        scratch_shapes=[pltpu.VMEM((width // 128, all_hours * group, 128), F32)],
        compiler_params=pltpu.CompilerParams(vmem_limit_bytes=40 * 2**20),
    )(core.reshape(all_hours * group, width))


def swap(values, axes):
    return lax.all_to_all(values, axes, 0, 0, tiled=True)


def spread_out(values, axes):
    count = lax.axis_size(axes)
    return swap(jnp.broadcast_to(values[None], (count,) + values.shape), axes)


def local(slab, start):
    cell_count, hour_count, kpi_count = slab.shape
    keep_count = start.shape[1]
    hour_devices = lax.axis_size(HOUR)
    near_devices = lax.axis_size(NEAR)
    all_cells = cell_count * lax.axis_size(("z_hi", "z_lo", "y"))
    all_hours = hour_count * hour_devices

    slab = jnp.transpose(slab, (1, 0, 2))
    partial_gram, slab = slab_gram(slab, 2, 1.0 / (all_cells * all_hours))
    pieces = partial_gram.reshape(near_devices, kpi_count // near_devices, kpi_count)
    piece = lax.psum(jnp.sum(swap(pieces, NEAR), axis=0), "z_lo")
    piece = lax.psum(lax.optimization_barrier(piece), "z_hi")
    kpi_gram = spread_out(piece, NEAR).reshape(kpi_count, kpi_count)

    subspace, core = subspace_and_core(kpi_gram, start.T, slab, hour_devices)
    core = swap(core, HOUR)
    parts = hour_gram_parts(core, hour_count, 1.0 / (all_cells * keep_count))
    rows = jnp.sum(swap(parts, HOUR), axis=0)
    rows = jnp.sum(spread_out(rows, ("z_lo", "y")), axis=0)
    hour_gram = lax.psum(rows, "z_hi")
    return subspace.T, hour_gram


def solution(mesh):
    fine = Mesh(
        mesh.devices.reshape(8, 4, 4, 4, 2), ("z_hi", "z_lo", "y", "x", "core")
    )
    return jax.shard_map(
        local,
        mesh=fine,
        in_specs=(P(("z_hi", "z_lo", "y"), HOUR, None), P()),
        out_specs=(P(), P(HOUR, None)),
        check_vma=False,
    )
```

```python
import functools

import jax
import jax.numpy as jnp
from jax import lax
from jax.experimental import pallas as pl
from jax.experimental.pallas import tpu as pltpu
from jax.sharding import Mesh, PartitionSpec as P

POWER = 2
F32 = jnp.float32
BF16 = jnp.bfloat16
HIGHEST = lax.Precision.HIGHEST
NEAR = ("y", "x", "core")
HOUR = ("x", "core")


def split(values):
    high = values.astype(BF16)
    low = (values - high.astype(F32)).astype(BF16)
    return high, low


def dot(a, b, contract):
    return lax.dot_general(a, b, (contract, ((), ())), preferred_element_type=F32)


def dot_full(a, b, contract):
    return lax.dot_general(
        a, b, (contract, ((), ())), precision=HIGHEST, preferred_element_type=F32
    )


def gram_kernel(scale, slab_ref, gram_ref, slab, sems):
    hours, cells, kpis = slab.shape
    count = sems.shape[0]
    step = hours // count
    copies = []
    for i in range(count):
        at = pl.ds(i * step, step)
        copies.append(pltpu.make_async_copy(slab_ref.at[at], slab.at[at], sems.at[i]))
        copies[-1].start()
    first = ((0,), (0,))
    even = jnp.zeros((kpis, kpis), F32)
    cross = jnp.zeros((kpis, kpis), F32)
    for i in range(count):
        at = pl.ds(i * step, step)
        copies[i].wait()
        high, low = split(slab[at].reshape(step * cells, kpis))
        cross += dot(high, low, first)
        even += dot(high, high, first) + dot(low, low, first)
    gram_ref[...] = (even + (cross + cross.T)) * scale


def slab_gram(slab, steps, scale):
    hours, cells, kpis = slab.shape
    return pl.pallas_call(
        functools.partial(gram_kernel, scale),
        in_specs=[pl.BlockSpec(memory_space=pl.ANY)],
        out_specs=[pl.BlockSpec(memory_space=pltpu.VMEM)] * 2,
        out_shape=[pltpu.VMEM((kpis, kpis), F32), pltpu.VMEM(slab.shape, F32)],
        scratch_shapes=[pltpu.SemaphoreType.DMA((steps,))],
        compiler_params=pltpu.CompilerParams(vmem_limit_bytes=58 * 2**20),
    )(slab)


def inverse_factor(gram):
    size = gram.shape[0]
    blocks = size // 8
    width = 2 * size
    row_index = lax.broadcasted_iota(jnp.int32, (size, size), 0)
    column_index = lax.broadcasted_iota(jnp.int32, (size, size), 1)
    identity = jnp.where(row_index == column_index, 1.0, 0.0).astype(F32)
    whole = jnp.concatenate([gram, identity], axis=1)
    work = [whole[8 * b : 8 * b + 8, :] for b in range(blocks)]
    sublane = lax.broadcasted_iota(jnp.int32, (8, width), 0)

    def fill(values):
        return jnp.broadcast_to(values, (8, width))

    def spread(panel):
        first = 8 * panel
        return {
            (k, b): fill(work[b][:, first + k : first + k + 1])
            for k in range(8)
            for b in range(panel, blocks)
        }

    now = spread(0)
    for panel in range(blocks):
        later = spread(panel + 1) if panel + 1 < blocks else {}
        for k in range(8):
            inverse = 1.0 / fill(now[k, panel][k : k + 1, :])
            pivots = {m: fill(now[m, panel][k : k + 1, :]) for m in range(k + 1, 8)}
            if later:
                next_pivots = [fill(now[k, panel + 1][m : m + 1, :]) for m in range(8)]
            row = fill(work[panel][k : k + 1, :])
            for b in range(panel, blocks):
                factor = now[k, b] * inverse
                if b == panel:
                    factor = jnp.where(sublane > k, factor, 0.0)
                for m in range(k + 1, 8):
                    now[m, b] = now[m, b] - factor * pivots[m]
                if b > panel:
                    for m in range(8):
                        later[m, b] = later[m, b] - factor * next_pivots[m]
                work[b] = work[b] - factor * row
        now = later
    whole = jnp.concatenate(work, axis=0)
    diagonal = jnp.sum(
        jnp.where(row_index == column_index, whole[:, :size], 0.0), axis=1, keepdims=True
    )
    return whole[:, size:] * lax.rsqrt(diagonal)


def near_inverse_factor(gram):
    size = gram.shape[0]
    row_index = lax.broadcasted_iota(jnp.int32, (size, size), 0)
    column_index = lax.broadcasted_iota(jnp.int32, (size, size), 1)
    identity = jnp.where(row_index == column_index, 1.0, 0.0).astype(F32)
    weight = jnp.where(row_index > column_index, 1.0, 0.0).astype(F32) + 0.5 * identity
    apart = gram - identity

    def series(_):
        once = (weight * apart).astype(BF16)
        twice = weight * (apart - dot(once, once, ((1,), (1,))))
        rounded = twice.astype(BF16)
        return identity - twice + dot(rounded, rounded, ((1,), (0,)))

    return lax.cond(
        jnp.sum(apart * apart) < 2.5e-5, series, lambda _: inverse_factor(gram), 0
    )


def orthonormalize(rows):
    for factor in (inverse_factor, near_inverse_factor):
        inner_gram = dot_full(rows, rows, ((1,), (1,)))
        rows = dot_full(factor(inner_gram), rows, ((1,), (0,)))
    return rows


def core_kernel(gram_ref, start_ref, slab_ref, subspace_ref, core_ref):
    gram = gram_ref[...]
    subspace = start_ref[...]
    for repeat in range(POWER):
        subspace = orthonormalize(dot_full(subspace, gram, ((1,), (0,))))
    subspace_ref[...] = subspace
    hours, cells, kpis = slab_ref.shape
    keep = subspace.shape[0]
    devices, _, group, width = core_ref.shape
    quarters = width // keep
    quarter = cells // quarters
    basis_high, basis_low = split(subspace)
    last = ((1,), (1,))
    none = jnp.zeros((keep, kpis), BF16)
    basis = jnp.concatenate(
        [
            jnp.concatenate(blocks, axis=1)
            for blocks in (
                (basis_high, none, basis_high, none),
                (none, basis_high, none, basis_high),
                (basis_low, none, none, none),
                (none, basis_low, none, none),
            )
        ],
        axis=0,
    )
    batch = 4
    for h in range(0, hours, batch):
        parts = []
        for q in range(0, quarters, 2):
            pair = []
            for side in (q, q + 1):
                at = pl.ds(side * quarter, quarter)
                pair.append(split(slab_ref[h : h + batch, at, :].reshape(batch * quarter, kpis)))
            columns = jnp.concatenate([pair[0][0], pair[1][0], pair[0][1], pair[1][1]], axis=1)
            both = dot(columns, basis, last)
            parts.append(both[:, : 2 * keep] + both[:, 2 * keep :])
        total = jnp.concatenate(parts, axis=1)
        for i in range(batch):
            for j in range(devices):
                at = i * quarter + j * group
                core_ref[j, h + i] = total[at : at + group]


def subspace_and_core(gram, start, slab, devices):
    hours, cells, kpis = slab.shape
    keep = start.shape[0]
    width = 256
    group = cells * keep // width // devices
    vmem = pl.BlockSpec(memory_space=pltpu.VMEM)
    return pl.pallas_call(
        core_kernel,
        in_specs=[vmem] * 3,
        out_specs=[vmem, vmem],
        out_shape=[
            jax.ShapeDtypeStruct((keep, kpis), F32),
            pltpu.VMEM((devices, hours, group, width), F32),
        ],
        compiler_params=pltpu.CompilerParams(vmem_limit_bytes=40 * 2**20),
    )(gram, start, slab)


def hour_kernel(hours, scale, core_ref, gram_ref, halves):
    group = 8
    rows, width = core_ref.shape
    lanes = halves.shape[2]
    for part in range(width // lanes):
        halves[part] = core_ref[:, part * lanes : (part + 1) * lanes]
    all_hours = rows // group
    devices = all_hours // hours
    total = jnp.zeros((all_hours, all_hours), F32)
    last = ((1,), (1,))
    for i in range(group):
        parts = [
            halves[part, pl.ds(i, all_hours, stride=group), :] for part in range(width // lanes)
        ]
        high, low = split(jnp.concatenate(parts, axis=1))
        cross = dot(high, low, last)
        total += dot(high, high, last) + dot(low, low, last) + (cross + cross.T)
    total = total * scale
    for d in range(devices):
        gram_ref[d] = total[d * hours : (d + 1) * hours, :]


def hour_gram_parts(core, hours, scale):
    group, width = core.shape[2:]
    all_hours = core.shape[0] * core.shape[1]
    vmem = pl.BlockSpec(memory_space=pltpu.VMEM)
    return pl.pallas_call(
        functools.partial(hour_kernel, hours, scale),
        in_specs=[vmem],
        out_specs=vmem,
        out_shape=jax.ShapeDtypeStruct((core.shape[0], hours, all_hours), F32),
        scratch_shapes=[pltpu.VMEM((width // 128, all_hours * group, 128), F32)],
        compiler_params=pltpu.CompilerParams(vmem_limit_bytes=40 * 2**20),
    )(core.reshape(all_hours * group, width))


def swap(values, axes):
    return lax.all_to_all(values, axes, 0, 0, tiled=True)


def spread_out(values, axes):
    count = lax.axis_size(axes)
    return swap(jnp.broadcast_to(values[None], (count,) + values.shape), axes)


def local(slab, start):
    cell_count, hour_count, kpi_count = slab.shape
    keep_count = start.shape[1]
    hour_devices = lax.axis_size(HOUR)
    near_devices = lax.axis_size(NEAR)
    all_cells = cell_count * lax.axis_size(("z_hi", "z_lo", "y"))
    all_hours = hour_count * hour_devices

    slab = jnp.transpose(slab, (1, 0, 2))
    partial_gram, slab = slab_gram(slab, 2, 1.0 / (all_cells * all_hours))
    pieces = partial_gram.reshape(near_devices, kpi_count // near_devices, kpi_count)
    piece = lax.psum(jnp.sum(swap(pieces, NEAR), axis=0), "z_lo")
    piece = lax.psum(lax.optimization_barrier(piece), "z_hi")
    kpi_gram = spread_out(piece, NEAR).reshape(kpi_count, kpi_count)

    subspace, core = subspace_and_core(kpi_gram, start.T, slab, hour_devices)
    core = swap(core, HOUR)
    parts = hour_gram_parts(core, hour_count, 1.0 / (all_cells * keep_count))
    rows = jnp.sum(swap(parts, HOUR), axis=0)
    rows = jnp.sum(spread_out(rows, ("z_lo", "y")), axis=0)
    hour_gram = lax.psum(rows, "z_hi")
    return subspace.T, hour_gram


def solution(mesh):
    fine = Mesh(
        mesh.devices.reshape(8, 4, 4, 4, 2), ("z_hi", "z_lo", "y", "x", "core")
    )
    return jax.shard_map(
        local,
        mesh=fine,
        in_specs=(P(("z_hi", "z_lo", "y"), HOUR, None), P()),
        out_specs=(P(), P(HOUR, None)),
        check_vma=False,
    )
```
